32 devices in a mesh: gx: 4 (over x, core), gy: 8 (over z, y).
Axes of the slice: x: 2, y: 2, z: 4, core: 2. Of those that a mesh axis runs over, the one named last changes fastest.
Arguments:
- fields_old: float32 [4096, 5, 512], P(('gx', 'gy')), may hold values from -6 to 6
- new_place: int32 [4096], P(('gx', 'gy')), may hold values from 0 to 4095, as said below
- box_slot: int32 [32, 128], P(('gx', 'gy')), may hold values from 0 to 127, each once within a row
- coarse_fields: float32 [1024, 5, 512], P(('gx', 'gy')), may hold values from -6 to 6
- coarse_source: int32 [32, 32], P(('gx', 'gy')), may hold values from 0 to 1023, as said below
- diffusivity: float32 [5], replicated, may hold values from 0.02 to 0.08
- velocity: float32 [3], replicated, may hold values from -0.15 to 0.15
Outputs:
- fields_new: float32 [4096, 5, 512], P(('gx', 'gy'))
The draws below stay inside these ranges and needn't reach their ends.
Inputs may be any that keep to these rules, and one draw needn't show every extreme that they name: `new_place`: A permutation of the patch numbers. One device sends at most 8 patches to any one device, and exactly 8 to some. `box_slot`: each row is a permutation. `coarse_source`: coarse patch c is held by device c // 32; the patches that a device names are held by the devices with its gy index; every coarse patch is named once over all devices; exactly 8 entries of a device name patches of each such owner.
All inputs are finite; a program needn't handle non-finite values.
Results may differ from the reference program's by a relative error of at most 0.00002.
Values sent between devices are 32-bit elements; how exact they have to be, the bound alone decides.
A program may use at most 128 MiB of HBM per device.

```python
import math
import jax
import jax.numpy as jnp

F = 5
S = 8
BX = 4
BY = 16
BZ = 2
SECTIONS = 4
P_DEV = 128
NEED = 32
CCAP = 8
NP = 4096
NC = 1024
N_GX = 4
N_GY = 8
DEVICES = 32


def row_permutations(key, rows, length):
    row_keys = jax.random.split(key, rows)
    return jax.vmap(lambda row_key: jax.random.permutation(row_key, length))(row_keys)


def circulant(key, devices, block_count):
    offsets = jax.random.permutation(jax.random.fold_in(key, 1), devices)[:block_count]
    relabel = jax.random.permutation(jax.random.fold_in(key, 2), devices)
    spread = jax.random.permutation(jax.random.fold_in(key, 3), devices)
    return relabel[(spread[:, None] + offsets[None, :]) % devices]


def assign(key, devices, per_device, capacity):
    block_count = per_device // capacity
    targets = circulant(jax.random.fold_in(key, 5), devices, block_count)
    receive_order = row_permutations(jax.random.fold_in(key, 6), devices, per_device)
    send_order = row_permutations(jax.random.fold_in(key, 7), devices, per_device)
    block_index = send_order // capacity
    within = send_order % capacity
    senders = jnp.arange(devices)[:, None]
    receivers = targets[senders, block_index]
    slot_index = receive_order[receivers, block_index * capacity + within]
    return (receivers * per_device + slot_index).astype(jnp.int32)


def draw_new_place(key, part):
    devices = NP // P_DEV
    return assign(jax.random.fold_in(key, 101), devices, P_DEV, 2 * P_DEV // devices).reshape(-1)


def draw_coarse_source(key, part):
    devices = NC // NEED
    column_count = NEED // CCAP
    row_count = devices // column_count
    owner_order = row_permutations(jax.random.fold_in(key, 301), devices, NEED)
    entry_order = row_permutations(jax.random.fold_in(key, 302), devices, NEED)
    shifts = jax.random.randint(jax.random.fold_in(key, 303), (row_count,), 0, column_count)
    owner_columns = jnp.arange(column_count, dtype=jnp.int32)
    inside = jnp.arange(CCAP, dtype=jnp.int32)

    def one_row(device):
        column = device // row_count
        row = device % row_count
        owner = owner_columns * row_count + row
        block = (column - owner_columns + shifts[row]) % column_count
        picks = owner_order[owner[:, None], block[:, None] * CCAP + inside[None, :]]
        names = (owner[:, None] * NEED + picks).reshape(-1)
        return names[entry_order[device]]
    return jax.vmap(one_row)(jnp.arange(devices, dtype=jnp.int32)).astype(jnp.int32)


def block_scale(own_key, dims, pieces, smallest, largest):
    def one(axis_at, blocks):
        steps = jax.random.uniform(jax.random.fold_in(jax.random.fold_in(own_key, 6), axis_at), (blocks,), jnp.float32, smallest / len(pieces), largest / len(pieces))
        return jnp.repeat(jnp.exp(steps), dims[axis_at] // blocks).reshape((-1,) + (1,) * (len(dims) - axis_at - 1))

    level = one(*pieces[0])
    for cut in pieces[1:]:
        level = level * one(*cut)
    return level


def noise(stream_key, dims, width, most, cuts=(), held_as=jnp.bfloat16):
    factor_of = block_scale(stream_key, dims, cuts, -0.22, 0.18) if cuts else 1.0
    drawn = jax.random.normal(stream_key, dims, jnp.float32) * width * factor_of
    return jnp.minimum(jnp.maximum(drawn, -most), most).astype(held_as)


def setup_inputs(seed: int = 0) -> dict:
    arg_keys = jax.random.split(jax.random.key(seed), 8)
    return {
        "fields_old": noise(arg_keys[0], (NP, F, S**3), 1.0, 6.0, ((0, 32),), jnp.float32),
        "new_place": draw_new_place(jax.random.fold_in(arg_keys[7], 71), 0),
        "box_slot": jax.vmap(lambda own: jax.random.permutation(own, P_DEV))(jax.random.split(arg_keys[2], DEVICES)).reshape((DEVICES, P_DEV)).astype(jnp.int32),
        "coarse_fields": noise(arg_keys[3], (NC, F, S**3), 1.0, 6.0, ((0, 32),), jnp.float32),
        "coarse_source": draw_coarse_source(jax.random.fold_in(arg_keys[7], 71), 0),
        "diffusivity": jnp.clip(jnp.exp(jax.random.uniform(arg_keys[5], (F,), jnp.float32, math.log(0.02), math.log(0.08))), 0.02, 0.08),
        "velocity": jnp.clip(jax.random.uniform(arg_keys[6], (3,), jnp.float32, -0.15, 0.15), -0.15, 0.15),
    }


def shifted(values, direction, offset):
    window = [slice(1, -1), slice(1, -1), slice(1, -1)]
    window[direction] = slice(offset, offset + values.shape[direction] - 2)
    return values[tuple(window)]


def update_field(padded, thermal, diffusivity, velocity):
    coefficient = diffusivity * thermal
    middle = shifted(padded, 0, 1)
    coef_mid = shifted(coefficient, 0, 1)
    updated = middle
    for direction in range(3):
        forward = shifted(padded, direction, 2)
        behind = shifted(padded, direction, 0)
        coef_up = shifted(coefficient, direction, 2)
        coef_down = shifted(coefficient, direction, 0)
        drift_speed = velocity[direction]
        updated = updated + 0.5 * (coef_mid + coef_up) * (forward - middle) - 0.5 * (coef_mid + coef_down) * (middle - behind)
        updated = updated - (jnp.maximum(drift_speed, 0.0) * (middle - behind) + jnp.minimum(drift_speed, 0.0) * (forward - middle))
    return updated


def global_grid(boxed_rows):
    blocks = boxed_rows.reshape(N_GX, N_GY, BZ, BX, BY, F, S, S, S)
    return blocks.transpose(5, 2, 6, 0, 3, 7, 1, 4, 8).reshape(F, BZ * S, N_GX * BX * S, N_GY * BY * S)


def global_rows(fine_grid):
    blocks = fine_grid.reshape(F, BZ, S, N_GX, BX, S, N_GY, BY, S)
    return blocks.transpose(3, 6, 1, 4, 7, 0, 2, 5, 8).reshape(NP, F, S * S * S)


def reference(fields_old, new_place, box_slot, coarse_fields, coarse_source, diffusivity, velocity):
    flat_boxes = box_slot.reshape(-1)
    owners = new_place // P_DEV
    position = owners * P_DEV + flat_boxes[new_place]
    boxed_rows = jnp.zeros(fields_old.shape, jnp.float32).at[position].set(fields_old)
    fine_grid = global_grid(boxed_rows)
    coarse_layered = coarse_fields.reshape(NC, F, S, S * S)
    is_upper = (jnp.arange(NEED, dtype=jnp.int32) >= NEED // 2)[None, :]
    is_upper = jnp.broadcast_to(is_upper, coarse_source.shape)
    near_layer = jnp.where(is_upper, 0, S - 1)
    far_layer = jnp.where(is_upper, 1, S - 2)
    nearest = coarse_layered[coarse_source, :, near_layer, :]
    farther = coarse_layered[coarse_source, :, far_layer, :]
    values = 1.25 * nearest - 0.25 * farther
    values = values.reshape(N_GX * N_GY, NEED, F, S, S)
    values = jnp.repeat(jnp.repeat(values, 2, axis=3), 2, axis=4)
    values = values.reshape(N_GX, N_GY, 2, BX // 2, BY // 2, F, 2 * S, 2 * S)
    planes = values.transpose(2, 5, 0, 3, 6, 1, 4, 7).reshape(2, F, N_GX * BX * S, N_GY * BY * S)
    cap_planes = jnp.pad(planes, ((0, 0), (0, 0), (1, 1), (1, 1)), mode="wrap")
    for section_no in range(SECTIONS):
        def padded_field(field_no):
            lateral = jnp.pad(fine_grid[field_no], ((0, 0), (1, 1), (1, 1)), mode="wrap")
            return jnp.concatenate([cap_planes[0, field_no][None], lateral, cap_planes[1, field_no][None]], axis=0)

        thermal = 1.0 + 0.5 * jnp.tanh(padded_field(0))
        results = []
        for field_no in range(F):
            results.append(update_field(padded_field(field_no), thermal, diffusivity[field_no], velocity))
        fine_grid = jnp.stack(results)
    rows_out = global_rows(fine_grid)
    slots = jnp.arange(NP, dtype=jnp.int32)
    return rows_out[(slots // P_DEV) * P_DEV + flat_boxes]
```

```python
import functools

import jax
import jax.numpy as jnp
from jax import lax
from jax.experimental import pallas as pl
from jax.experimental.pallas import tpu as pltpu
from jax.sharding import PartitionSpec as P

S = 8
BX = 4
BY = 16
BZ = 2
SECTIONS = 4
F = 5
LANES = BX * BY * BZ
LAYER = S * S
CHUNKS = S * LAYER // LANES
VMEM_LIMIT = 56 * 1024 * 1024
MESH = pl.DeviceIdType.MESH
NN = (((1,), (0,)), ((), ()))
TN = (((0,), (0,)), ((), ()))
NT = (((1,), (1,)), ((), ()))


def iota(shape, axis):
    return lax.broadcasted_iota(jnp.int32, shape, axis)


def one_hot(mask):
    return jnp.where(mask, 1.0, 0.0).astype(jnp.bfloat16)


def parts(value):
    high = value.astype(jnp.bfloat16)
    rest = value - high.astype(jnp.float32)
    middle = rest.astype(jnp.bfloat16)
    low = (rest - middle.astype(jnp.float32)).astype(jnp.bfloat16)
    return high, middle, low


def pick(left, right, dims):
    def dot(a, b):
        return lax.dot_general(a, b, dims, preferred_element_type=jnp.float32)

    if left.dtype == jnp.float32:
        high, middle, low = (dot(part, right) for part in parts(left))
    else:
        high, middle, low = (dot(left, part) for part in parts(right))
    return high + middle + low


def roll(value, shift, axis):
    size = value.shape[axis]
    shift = shift % size
    return value if shift == 0 else pltpu.roll(value, shift, axis)


def pack_kernel(capacity, x_ref, row_ref, col_ref, send_ref):
    patches = x_ref.shape[0]
    slots = send_ref.shape[1]
    bits = patches.bit_length() - 1
    row, col = row_ref[...], col_ref[...]
    dest_row = lax.shift_right_logical(row, bits)
    dest_col = lax.shift_right_logical(col, bits)
    square = (patches, patches)
    before = (dest_col == dest_row) & (iota(square, 0) < iota(square, 1))
    count = jnp.sum(jnp.where(before, 1, 0), axis=0, keepdims=True)
    position = dest_row * capacity + count
    chosen = iota((slots, patches), 0) == position
    tag = ((row & (patches - 1)) + 1).astype(jnp.float32)
    tags = jnp.sum(jnp.where(chosen, tag, 0.0), axis=1, keepdims=True)
    send_ref[F * CHUNKS] = jnp.broadcast_to(tags, (slots, LANES))
    matrix = one_hot(chosen)
    for f in range(F):
        moved = pick(matrix, x_ref[:, f, :], NN)
        for c in range(CHUNKS):
            send_ref[f * CHUNKS + c] = moved[:, c * LANES : (c + 1) * LANES]


def sections_kernel(
    recv_ref, lane_ref, wall_ref, cand_ref, diff_ref, vel_ref, out_ref,
    cells, caps, cap_heat, grid_a, grid_b, heat,
    send_x, recv_x, send_y, recv_y, send_sem, recv_sem,
):
    gx, gy = lax.axis_index("gx"), lax.axis_index("gy")
    nx, ny = lax.axis_size("gx"), lax.axis_size("gy")
    right = (lax.rem(gx + 1, nx), gy)
    left = (lax.rem(gx + nx - 1, nx), gy)
    ahead = (gx, lax.rem(gy + 1, ny))
    behind = (gx, lax.rem(gy + ny - 1, ny))
    barrier = pltpu.get_barrier_semaphore()
    for other in (right, left, ahead, behind):
        pl.semaphore_signal(barrier, inc=1, device_id=other, device_id_type=MESH)

    slots = recv_ref.shape[1]
    lane = iota((S, LANES), 1)
    by = lane & (BY - 1)
    bz = lax.shift_right_logical(lane, 4) & 1
    bx = lax.shift_right_logical(lane, 5)
    level = iota((S, LANES), 0)

    tag_lane = (iota((slots, LANES), 1) + 1).astype(jnp.float32)
    tagged = one_hot(recv_ref[F * CHUNKS] == tag_lane)
    boxed = one_hot(lane_ref[...] == iota((LANES, LANES), 1))
    place = lax.dot_general(
        tagged, boxed, NN, preferred_element_type=jnp.float32
    ).astype(jnp.bfloat16)
    for f in range(F):
        for c in range(CHUNKS):
            cells[f, c * LANES : (c + 1) * LANES, :] = pick(
                recv_ref[f * CHUNKS + c], place, TN
            )
        for jk in range(LAYER):
            grid_a[f, jk // S + 1, jk % S + 1] = cells[f, pl.ds(jk, S, stride=LAYER), :]
    candidates = wall_ref.shape[1]
    named = one_hot(iota((candidates, LANES), 0) == cand_ref[...])
    row_lane = iota((1, LANES), 1)
    odd_y = (row_lane & 1) == 1
    odd_x = (lax.shift_right_logical(row_lane, 5) & 1) == 1
    top = (lax.shift_right_logical(row_lane, 4) & 1) == 1
    for f in range(F):
        both = pick(wall_ref[f], named, TN)
        side = jnp.where(top, both[LAYER:], both[:LAYER])
        half = jnp.where(odd_x, side[LAYER // 2 :], side[: LAYER // 2])
        for j2 in range(S // 2):
            for k2 in range(S // 2):
                at = j2 * S + k2
                row = jnp.where(odd_y, half[at + 4 : at + 5], half[at : at + 1])
                full = jnp.broadcast_to(row, (S, LANES))
                caps[f, j2, 2 * k2] = full
                caps[f, j2, 2 * k2 + 1] = full
    cap_heat[...] = 1.0 + 0.5 * jnp.tanh(caps[0])
    for a in (0, S + 1):
        for b in (0, S + 1):
            grid_a[0, a, b] = jnp.zeros((S, LANES), jnp.float32)
            grid_b[0, a, b] = jnp.zeros((S, LANES), jnp.float32)

    pl.semaphore_wait(barrier, 4)

    started = []
    for section in range(SECTIONS):
        now, later = (grid_a, grid_b) if section % 2 == 0 else (grid_b, grid_a)
        copies = []

        def send(src, dst, way, target):
            copy = pltpu.make_async_remote_copy(
                src_ref=src.at[section, way % 2],
                dst_ref=dst.at[section, way % 2],
                send_sem=send_sem.at[section, way],
                recv_sem=recv_sem.at[section, way],
                device_id=target,
                device_id_type=MESH,
            )
            copy.start()
            copies.append(copy)
            started.append(copy)

        for way, column, edge, target in ((2, S, BY - 1, ahead), (3, 1, 0, behind)):
            for q in range(-(-F * S // BY)):
                packed = jnp.zeros((S, LANES), jnp.float32)
                for r in range(BY):
                    n = q * BY + r
                    if n < F * S:
                        face = now[n // S, n % S + 1, column]
                        packed = jnp.where(by == r, roll(face, r - edge, 1), packed)
                send_y[section, way - 2, q] = packed
            send(send_y, recv_y, way, target)
        for way, plane, edge, target in ((0, S, BX - 1, right), (1, 1, 0, left)):
            for f in range(F):
                for q in range(S // BX):
                    packed = jnp.zeros((S, LANES), jnp.float32)
                    for g in range(BX):
                        face = now[f, plane, q * BX + g + 1]
                        moved = roll(face, (g - edge) * BY * BZ, 1)
                        packed = jnp.where(bx == g, moved, packed)
                    send_x[section, way, f * (S // BX) + q] = packed
            send(send_x, recv_x, way, target)

        for order, (way, column, target_column, edge, step) in enumerate(
            ((0, S, 0, 0, 1), (1, 1, S + 1, BY - 1, -1))
        ):
            copies[order].wait_recv()
            for n in range(F * S):
                q, r = n // BY, n % BY
                remote = roll(recv_y[section, way, q], edge - r, 1)
                local = roll(now[n // S, n % S + 1, column], step, 1)
                now[n // S, n % S + 1, target_column] = jnp.where(by == edge, remote, local)
        for order, (way, plane, target_plane, edge, step) in enumerate(
            ((0, S, 0, 0, 1), (1, 1, S + 1, BX - 1, -1))
        ):
            copies[2 + order].wait_recv()
            for f in range(F):
                for k in range(S):
                    q, g = k // BX, k % BX
                    packed = recv_x[section, way, f * (S // BX) + q]
                    remote = roll(packed, (edge - g) * BY * BZ, 1)
                    local = roll(now[f, plane, k + 1], step * BY * BZ, 1)
                    now[f, target_plane, k + 1] = jnp.where(bx == edge, remote, local)

        def warm(j, carry):
            heat[j] = 1.0 + 0.5 * jnp.tanh(now[0, j])
            return carry

        lax.fori_loop(0, S + 2, warm, 0)

        box = (S, S, LANES)
        is_top = (iota(box, 1) == S - 1)
        is_bottom = (iota(box, 1) == 0)
        bz3 = lax.shift_right_logical(iota(box, 2), 4) & 1

        def neighbours(value, cap):
            rolled = roll(value, -1, 1)
            outer = jnp.where(bz3 == 0, roll(rolled, -BY, 2), cap)
            above = jnp.where(is_top, outer, rolled)
            rolled = roll(value, 1, 1)
            outer = jnp.where(bz3 == 1, roll(rolled, BY, 2), cap)
            below = jnp.where(is_bottom, outer, rolled)
            return above, below

        def pair(j2, carry):
            for jr in range(2):
                j = 2 * j2 + jr + 1
                inner = slice(1, S + 1)
                here = heat[j, inner]
                warm_z = neighbours(here, cap_heat[j2])
                warm_x = heat[j + 1, inner], heat[j - 1, inner]
                warm_y = heat[j, 2 : S + 2], heat[j, 0:S]
                means = [
                    (0.5 * (here + up), 0.5 * (here + down))
                    for up, down in (warm_z, warm_x, warm_y)
                ]
                for f in range(F):
                    u = now[f, j, inner]
                    around = (
                        neighbours(u, caps[f, j2]),
                        (now[f, j + 1, inner], now[f, j - 1, inner]),
                        (now[f, j, 2 : S + 2], now[f, j, 0:S]),
                    )
                    total = u
                    for axis in range(3):
                        up, down = around[axis]
                        mean_up, mean_down = means[axis]
                        v = vel_ref[axis]
                        total = total + (diff_ref[f] * mean_up - jnp.minimum(v, 0.0)) * (up - u)
                        total = total - (diff_ref[f] * mean_down + jnp.maximum(v, 0.0)) * (u - down)
                    if section == SECTIONS - 1:
                        out_ref[f, j - 1] = total
                    else:
                        later[f, j, inner] = total
            return carry

        lax.fori_loop(0, S // 2, pair, 0)
    for copy in started:
        copy.wait_send()


def rows_kernel(grid_ref, lane_ref, out_ref):
    patches = lane_ref.shape[0]
    boxed = one_hot(lane_ref[...] == iota((patches, LANES), 1))
    for f in range(F):
        for c in range(CHUNKS):
            per = LANES // LAYER
            cells = jnp.concatenate(
                [grid_ref[f, pl.ds(c * per + i, LAYER, stride=S), :] for i in range(per)],
                axis=0,
            )
            out_ref[:, f, c * LANES : (c + 1) * LANES] = pick_rows(boxed, cells)


def pick_rows(boxed, cells):
    return pick(boxed, cells, NT)


def vmem(count):
    return [pl.BlockSpec(memory_space=pltpu.VMEM)] * count


def per_device(
    fields_old, new_place, box_slot, coarse_fields, coarse_source, diffusivity, velocity
):
    devices = lax.axis_size(("gx", "gy"))
    mesh_x = lax.axis_size("gx")
    mesh_y = lax.axis_size("gy")
    patches = fields_old.shape[0]
    capacity = 2 * patches // devices
    slots = devices * capacity
    tiles = F * CHUNKS + 1
    need = coarse_source.shape[1]
    f32 = jnp.float32

    packed = pl.pallas_call(
        functools.partial(pack_kernel, capacity),
        out_shape=jax.ShapeDtypeStruct((tiles, slots, LANES), f32),
        in_specs=vmem(3),
        out_specs=vmem(1)[0],
        compiler_params=pltpu.CompilerParams(vmem_limit_bytes=VMEM_LIMIT),
        name="pack",
    )(fields_old, new_place.reshape(1, patches), new_place.reshape(patches, 1))
    arrived = lax.all_to_all(packed, ("gx", "gy"), split_axis=1, concat_axis=1, tiled=True)

    top = S * LAYER
    below = 1.25 * coarse_fields[:, :, top - LAYER :] - 0.25 * coarse_fields[:, :, top - 2 * LAYER : top - LAYER]
    above = 1.25 * coarse_fields[:, :, :LAYER] - 0.25 * coarse_fields[:, :, LAYER : 2 * LAYER]
    walls = jnp.concatenate([below, above], axis=2).transpose(1, 0, 2)
    walls = lax.all_gather(walls, "gx", axis=1, tiled=True)

    box = box_slot[0]
    lane = ((box >> 4) & 3) * (BY * BZ) + (box >> 6) * BY + (box & 15)
    lane = lane.reshape(patches, 1)
    source = coarse_source[0]
    candidate = (source // need // mesh_y) * need + source % need
    candidate = candidate.reshape(2, BX // 2, BY // 2).transpose(1, 0, 2)
    candidate = jnp.broadcast_to(
        candidate[:, None, :, :, None], (BX // 2, 2, 2, BY // 2, 2)
    ).reshape(1, LANES)

    dma = pltpu.SemaphoreType.DMA((SECTIONS, 4))
    padded = pltpu.VMEM((F, S + 2, S + 2, S, LANES), f32)
    faces_x = pltpu.VMEM((SECTIONS, 2, F * S // BX, S, LANES), f32)
    faces_y = pltpu.VMEM((SECTIONS, 2, -(-F * S // BY), S, LANES), f32)
    smem = pl.BlockSpec(memory_space=pltpu.SMEM)
    grid = pl.pallas_call(
        sections_kernel,
        out_shape=jax.ShapeDtypeStruct((F, S, S, S, LANES), f32),
        in_specs=vmem(4) + [smem, smem],
        out_specs=vmem(1)[0],
        scratch_shapes=[
            pltpu.VMEM((F, S * LAYER, LANES), f32),
            pltpu.VMEM((F, S // 2, S, S, LANES), f32),
            pltpu.VMEM((S // 2, S, S, LANES), f32),
            padded,
            padded,
            pltpu.VMEM((S + 2, S + 2, S, LANES), f32),
            faces_x,
            faces_x,
            faces_y,
            faces_y,
            dma,
            dma,
        ],
        compiler_params=pltpu.CompilerParams(
            collective_id=1, has_side_effects=True, vmem_limit_bytes=VMEM_LIMIT
        ),
        name="sections",
    )(arrived, lane, walls, candidate, diffusivity, velocity)
    return pl.pallas_call(
        rows_kernel,
        out_shape=jax.ShapeDtypeStruct(fields_old.shape, f32),
        in_specs=vmem(2),
        out_specs=vmem(1)[0],
        compiler_params=pltpu.CompilerParams(vmem_limit_bytes=VMEM_LIMIT),
        name="rows",
    )(grid.reshape(F, LAYER * S, LANES), lane)


def solution(mesh):
    in_specs = (
        P(("gx", "gy"), None, None),
        P(("gx", "gy")),
        P(("gx", "gy"), None),
        P(("gx", "gy"), None, None),
        P(("gx", "gy"), None),
        P(),
        P(),
    )
    out_specs = P(("gx", "gy"), None, None)
    return jax.shard_map(
        per_device, mesh=mesh, in_specs=in_specs, out_specs=out_specs, check_vma=False
    )
```

```python
import functools

import jax
import jax.numpy as jnp
from jax import lax
from jax.experimental import pallas as pl
from jax.experimental.pallas import tpu as pltpu
from jax.sharding import PartitionSpec as P

S = 8
BX = 4
BY = 16
BZ = 2
SECTIONS = 4
F = 5
LANES = BX * BY * BZ
LAYER = S * S
CHUNKS = S * LAYER // LANES
VMEM_LIMIT = 56 * 1024 * 1024
MESH = pl.DeviceIdType.MESH
NN = (((1,), (0,)), ((), ()))
TN = (((0,), (0,)), ((), ()))
NT = (((1,), (1,)), ((), ()))


def iota(shape, axis):
    return lax.broadcasted_iota(jnp.int32, shape, axis)


def one_hot(mask):
    return jnp.where(mask, 1.0, 0.0).astype(jnp.bfloat16)


def parts(value):
    high = value.astype(jnp.bfloat16)
    rest = value - high.astype(jnp.float32)
    middle = rest.astype(jnp.bfloat16)
    low = (rest - middle.astype(jnp.float32)).astype(jnp.bfloat16)
    return high, middle, low


def pick(left, right, dims):
    def dot(a, b):
        return lax.dot_general(a, b, dims, preferred_element_type=jnp.float32)

    if left.dtype == jnp.float32:
        high, middle, low = (dot(part, right) for part in parts(left))
    else:
        high, middle, low = (dot(left, part) for part in parts(right))
    return high + middle + low


def roll(value, shift, axis):
    size = value.shape[axis]
    shift = shift % size
    return value if shift == 0 else pltpu.roll(value, shift, axis)


def slot_matrix(capacity, slots, row, col):
    patches = row.shape[1]
    bits = patches.bit_length() - 1
    dest_row = lax.shift_right_logical(row, bits)
    dest_col = lax.shift_right_logical(col, bits)
    square = (patches, patches)
    before = (dest_col == dest_row) & (iota(square, 0) < iota(square, 1))
    count = jnp.sum(jnp.where(before, 1, 0), axis=0, keepdims=True)
    position = dest_row * capacity + count
    chosen = iota((slots, patches), 0) == position
    tag = ((row & (patches - 1)) + 1).astype(jnp.float32)
    tags = jnp.sum(jnp.where(chosen, tag, 0.0), axis=1, keepdims=True)
    return one_hot(chosen), jnp.broadcast_to(tags, (slots, LANES))


def pack(capacity, x_ref, row_ref, col_ref, send_ref):
    devices = send_ref.shape[0]
    block = (devices, capacity, LANES)
    matrix, tags = slot_matrix(capacity, devices * capacity, row_ref[...], col_ref[...])
    send_ref[:, F * CHUNKS] = tags.reshape(block)
    for f in range(F):
        moved = pick(matrix, x_ref[f], NN)
        for c in range(CHUNKS):
            send_ref[:, f * CHUNKS + c] = moved[:, c * LANES : (c + 1) * LANES].reshape(block)


def layers(coarse_ref, f):
    low = coarse_ref[f, :, :LANES]
    high = coarse_ref[f, :, (CHUNKS - 1) * LANES :]
    below = 1.25 * roll(high, LAYER, 1) - 0.25 * high
    above = 1.25 * roll(low, LAYER, 1) - 0.25 * low
    return jnp.where(iota(low.shape, 1) < LAYER, below, above)


def pack_kernel(capacity, x_ref, row_ref, col_ref, coarse_ref, send_ref, wall_ref):
    pack(capacity, x_ref, row_ref, col_ref, send_ref)
    for f in range(F):
        wall_ref[f] = layers(coarse_ref, f)


def exchange_kernel(
    capacity, x_ref, row_ref, col_ref, coarse_ref, recv_ref, walls_ref,
    send, wall, send_sem, recv_sem, wall_send, wall_recv, local_sem,
):
    gx, gy = lax.axis_index("gx"), lax.axis_index("gy")
    nx, ny = lax.axis_size("gx"), lax.axis_size("gy")
    devices = nx * ny
    me = gx * ny + gy
    barrier = pltpu.get_barrier_semaphore()

    def partner(k):
        other = me ^ k
        return other, (lax.div(other, ny), lax.rem(other, ny))

    def greet(k, carry):
        pl.semaphore_signal(barrier, inc=1, device_id=partner(k)[1], device_id_type=MESH)
        return carry

    lax.fori_loop(1, devices, greet, 0)
    for f in range(F):
        wall[f] = layers(coarse_ref, f)
    pack(capacity, x_ref, row_ref, col_ref, send)
    pl.semaphore_wait(barrier, devices - 1)

    def message(k):
        other, where = partner(k)
        return pltpu.make_async_remote_copy(
            src_ref=send.at[other],
            dst_ref=recv_ref.at[me],
            send_sem=send_sem.at[k],
            recv_sem=recv_sem.at[k],
            device_id=where,
            device_id_type=MESH,
        )

    def wall_message(k):
        return pltpu.make_async_remote_copy(
            src_ref=wall,
            dst_ref=walls_ref.at[gx],
            send_sem=wall_send.at[k],
            recv_sem=wall_recv.at[k],
            device_id=(gx ^ k, gy),
            device_id_type=MESH,
        )

    def begin(k, carry):
        message(k).start()
        return carry

    lax.fori_loop(1, devices, begin, 0)
    own = pltpu.make_async_copy(send.at[me], recv_ref.at[me], local_sem.at[0])
    own_wall = pltpu.make_async_copy(wall, walls_ref.at[gx], local_sem.at[1])
    own.start()
    own_wall.start()
    for k in range(1, nx):
        wall_message(k).start()
    for k in range(1, nx):
        wall_message(k).wait()

    def finish(k, carry):
        message(k).wait()
        return carry

    lax.fori_loop(1, devices, finish, 0)
    own.wait()
    own_wall.wait()


def sections_kernel(
    recv_ref, lane_ref, wall_ref, cand_ref, diff_ref, vel_ref, out_ref,
    cells, caps, cap_heat, grid_a, grid_b, heat,
    send_x, recv_x, send_y, recv_y, send_sem, recv_sem,
):
    gx, gy = lax.axis_index("gx"), lax.axis_index("gy")
    nx, ny = lax.axis_size("gx"), lax.axis_size("gy")
    right = (lax.rem(gx + 1, nx), gy)
    left = (lax.rem(gx + nx - 1, nx), gy)
    ahead = (gx, lax.rem(gy + 1, ny))
    behind = (gx, lax.rem(gy + ny - 1, ny))
    barrier = pltpu.get_barrier_semaphore()
    for other in (right, left, ahead, behind):
        pl.semaphore_signal(barrier, inc=1, device_id=other, device_id_type=MESH)

    slots = recv_ref.shape[0] * recv_ref.shape[2]
    lane = iota((S, LANES), 1)
    by = lane & (BY - 1)
    bz = lax.shift_right_logical(lane, 4) & 1
    bx = lax.shift_right_logical(lane, 5)
    level = iota((S, LANES), 0)

    tag_lane = (iota((slots, LANES), 1) + 1).astype(jnp.float32)
    tagged = one_hot(recv_ref[:, F * CHUNKS].reshape(slots, LANES) == tag_lane)
    boxed = one_hot(lane_ref[...] == iota((LANES, LANES), 1))
    place = lax.dot_general(tagged, boxed, NN, preferred_element_type=jnp.float32)
    place = place.T.astype(jnp.bfloat16)
    for f in range(F):
        for c in range(CHUNKS):
            rows = recv_ref[:, f * CHUNKS + c].reshape(slots, LANES)
            cells[f, c * LANES : (c + 1) * LANES, :] = pick(place, rows, NN).T
        for jk in range(LAYER):
            grid_a[f, jk // S + 1, jk % S + 1] = cells[f, pl.ds(jk, S, stride=LAYER), :]
    candidates = wall_ref.shape[0] * wall_ref.shape[2]
    named = one_hot(iota((candidates, LANES), 0) == cand_ref[...])
    row_lane = iota((1, LANES), 1)
    odd_y = (row_lane & 1) == 1
    odd_x = (lax.shift_right_logical(row_lane, 5) & 1) == 1
    top = (lax.shift_right_logical(row_lane, 4) & 1) == 1
    for f in range(F):
        both = pick(wall_ref[:, f].reshape(candidates, LANES), named, TN)
        side = jnp.where(top, both[LAYER:], both[:LAYER])
        half = jnp.where(odd_x, side[LAYER // 2 :], side[: LAYER // 2])
        for j2 in range(S // 2):
            for k2 in range(S // 2):
                at = j2 * S + k2
                row = jnp.where(odd_y, half[at + 4 : at + 5], half[at : at + 1])
                full = jnp.broadcast_to(row, (S, LANES))
                caps[f, j2, 2 * k2] = full
                caps[f, j2, 2 * k2 + 1] = full
    cap_heat[...] = 1.0 + 0.5 * jnp.tanh(caps[0])
    for a in (0, S + 1):
        for b in (0, S + 1):
            grid_a[0, a, b] = jnp.zeros((S, LANES), jnp.float32)
            grid_b[0, a, b] = jnp.zeros((S, LANES), jnp.float32)

    pl.semaphore_wait(barrier, 4)

    started = []
    for section in range(SECTIONS):
        now, later = (grid_a, grid_b) if section % 2 == 0 else (grid_b, grid_a)
        copies = []

        def send(src, dst, way, target):
            copy = pltpu.make_async_remote_copy(
                src_ref=src.at[section, way % 2],
                dst_ref=dst.at[section, way % 2],
                send_sem=send_sem.at[section, way],
                recv_sem=recv_sem.at[section, way],
                device_id=target,
                device_id_type=MESH,
            )
            copy.start()
            copies.append(copy)
            started.append(copy)

        for way, column, edge, target in ((2, S, BY - 1, ahead), (3, 1, 0, behind)):
            for q in range(-(-F * S // BY)):
                packed = jnp.zeros((S, LANES), jnp.float32)
                for r in range(BY):
                    n = q * BY + r
                    if n < F * S:
                        face = now[n // S, n % S + 1, column]
                        packed = jnp.where(by == r, roll(face, r - edge, 1), packed)
                send_y[section, way - 2, q] = packed
            send(send_y, recv_y, way, target)
        for way, plane, edge, target in ((0, S, BX - 1, right), (1, 1, 0, left)):
            for f in range(F):
                for q in range(S // BX):
                    packed = jnp.zeros((S, LANES), jnp.float32)
                    for g in range(BX):
                        face = now[f, plane, q * BX + g + 1]
                        moved = roll(face, (g - edge) * BY * BZ, 1)
                        packed = jnp.where(bx == g, moved, packed)
                    send_x[section, way, f * (S // BX) + q] = packed
            send(send_x, recv_x, way, target)

        for order, (way, column, target_column, edge, step) in enumerate(
            ((0, S, 0, 0, 1), (1, 1, S + 1, BY - 1, -1))
        ):
            copies[order].wait_recv()
            for n in range(F * S):
                q, r = n // BY, n % BY
                remote = roll(recv_y[section, way, q], edge - r, 1)
                local = roll(now[n // S, n % S + 1, column], step, 1)
                now[n // S, n % S + 1, target_column] = jnp.where(by == edge, remote, local)
        for order, (way, plane, target_plane, edge, step) in enumerate(
            ((0, S, 0, 0, 1), (1, 1, S + 1, BX - 1, -1))
        ):
            copies[2 + order].wait_recv()
            for f in range(F):
                for k in range(S):
                    q, g = k // BX, k % BX
                    packed = recv_x[section, way, f * (S // BX) + q]
                    remote = roll(packed, (edge - g) * BY * BZ, 1)
                    local = roll(now[f, plane, k + 1], step * BY * BZ, 1)
                    now[f, target_plane, k + 1] = jnp.where(bx == edge, remote, local)

        def warm(j, carry):
            heat[j] = 1.0 + 0.5 * jnp.tanh(now[0, j])
            return carry

        lax.fori_loop(0, S + 2, warm, 0)

        box = (S, S, LANES)
        is_top = (iota(box, 1) == S - 1)
        is_bottom = (iota(box, 1) == 0)
        bz3 = lax.shift_right_logical(iota(box, 2), 4) & 1

        def neighbours(value, cap):
            rolled = roll(value, -1, 1)
            outer = jnp.where(bz3 == 0, roll(rolled, -BY, 2), cap)
            above = jnp.where(is_top, outer, rolled)
            rolled = roll(value, 1, 1)
            outer = jnp.where(bz3 == 1, roll(rolled, BY, 2), cap)
            below = jnp.where(is_bottom, outer, rolled)
            return above, below

        def pair(j2, carry):
            for jr in range(2):
                j = 2 * j2 + jr + 1
                inner = slice(1, S + 1)
                here = heat[j, inner]
                warm_z = neighbours(here, cap_heat[j2])
                warm_x = heat[j + 1, inner], heat[j - 1, inner]
                warm_y = heat[j, 2 : S + 2], heat[j, 0:S]
                means = [
                    (0.5 * (here + up), 0.5 * (here + down))
                    for up, down in (warm_z, warm_x, warm_y)
                ]
                for f in range(F):
                    u = now[f, j, inner]
                    around = (
                        neighbours(u, caps[f, j2]),
                        (now[f, j + 1, inner], now[f, j - 1, inner]),
                        (now[f, j, 2 : S + 2], now[f, j, 0:S]),
                    )
                    total = u
                    for axis in range(3):
                        up, down = around[axis]
                        mean_up, mean_down = means[axis]
                        v = vel_ref[axis]
                        total = total + (diff_ref[f] * mean_up - jnp.minimum(v, 0.0)) * (up - u)
                        total = total - (diff_ref[f] * mean_down + jnp.maximum(v, 0.0)) * (u - down)
                    if section == SECTIONS - 1:
                        out_ref[f, j - 1] = total
                    else:
                        later[f, j, inner] = total
            return carry

        lax.fori_loop(0, S // 2, pair, 0)
    for copy in started:
        copy.wait_send()


def rows_kernel(grid_ref, lane_ref, out_ref):
    patches = lane_ref.shape[0]
    boxed = one_hot(lane_ref[...] == iota((patches, LANES), 1))
    for f in range(F):
        for c in range(CHUNKS):
            per = LANES // LAYER
            cells = jnp.concatenate(
                [grid_ref[f, pl.ds(c * per + i, LAYER, stride=S), :] for i in range(per)],
                axis=0,
            )
            out_ref[f, :, c * LANES : (c + 1) * LANES] = pick(boxed, cells, NT)


def vmem(count):
    return [pl.BlockSpec(memory_space=pltpu.VMEM)] * count


def per_device(
    fields_old, new_place, box_slot, coarse_fields, coarse_source, diffusivity, velocity
):
    devices = lax.axis_size(("gx", "gy"))
    mesh_x = lax.axis_size("gx")
    mesh_y = lax.axis_size("gy")
    patches = fields_old.shape[0]
    capacity = 2 * patches // devices
    tiles = F * CHUNKS + 1
    need = coarse_source.shape[1]
    f32 = jnp.float32

    own = need
    operands = (
        fields_old.transpose(1, 0, 2),
        new_place.reshape(1, patches),
        new_place.reshape(patches, 1),
        coarse_fields.transpose(1, 0, 2),
    )
    if capacity % 8 == 0 and devices & (devices - 1) == 0 and mesh_x & (mesh_x - 1) == 0:
        any_space = pl.BlockSpec(memory_space=pl.ANY)
        block = (devices, tiles, capacity, LANES)
        arrived, walls = pl.pallas_call(
            functools.partial(exchange_kernel, capacity),
            out_shape=(
                jax.ShapeDtypeStruct(block, f32),
                jax.ShapeDtypeStruct((mesh_x, F, own, LANES), f32),
            ),
            in_specs=vmem(4),
            out_specs=(any_space, any_space),
            scratch_shapes=[
                pltpu.VMEM(block, f32),
                pltpu.VMEM((F, own, LANES), f32),
                pltpu.SemaphoreType.DMA((devices,)),
                pltpu.SemaphoreType.DMA((devices,)),
                pltpu.SemaphoreType.DMA((mesh_x,)),
                pltpu.SemaphoreType.DMA((mesh_x,)),
                pltpu.SemaphoreType.DMA((2,)),
            ],
            compiler_params=pltpu.CompilerParams(
                collective_id=2, has_side_effects=True, vmem_limit_bytes=VMEM_LIMIT
            ),
            name="exchange",
        )(*operands)
    else:
        packed, walls = pl.pallas_call(
            functools.partial(pack_kernel, capacity),
            out_shape=(
                jax.ShapeDtypeStruct((devices, tiles, capacity, LANES), f32),
                jax.ShapeDtypeStruct((F, own, LANES), f32),
            ),
            in_specs=vmem(4),
            out_specs=tuple(vmem(2)),
            compiler_params=pltpu.CompilerParams(vmem_limit_bytes=VMEM_LIMIT),
            name="pack",
        )(*operands)
        arrived = lax.all_to_all(packed, ("gx", "gy"), split_axis=0, concat_axis=0, tiled=True)
        walls = lax.all_gather(walls, "gx", axis=0)

    box = box_slot[0]
    lane = ((box >> 4) & 3) * (BY * BZ) + (box >> 6) * BY + (box & 15)
    lane = lane.reshape(patches, 1)
    source = coarse_source[0]
    candidate = (source // need // mesh_y) * need + source % need
    candidate = candidate.reshape(2, BX // 2, BY // 2).transpose(1, 0, 2)
    candidate = jnp.broadcast_to(
        candidate[:, None, :, :, None], (BX // 2, 2, 2, BY // 2, 2)
    ).reshape(1, LANES)

    dma = pltpu.SemaphoreType.DMA((SECTIONS, 4))
    padded = pltpu.VMEM((F, S + 2, S + 2, S, LANES), f32)
    faces_x = pltpu.VMEM((SECTIONS, 2, F * S // BX, S, LANES), f32)
    faces_y = pltpu.VMEM((SECTIONS, 2, -(-F * S // BY), S, LANES), f32)
    smem = pl.BlockSpec(memory_space=pltpu.SMEM)
    grid = pl.pallas_call(
        sections_kernel,
        out_shape=jax.ShapeDtypeStruct((F, S, S, S, LANES), f32),
        in_specs=vmem(4) + [smem, smem],
        out_specs=vmem(1)[0],
        scratch_shapes=[
            pltpu.VMEM((F, S * LAYER, LANES), f32),
            pltpu.VMEM((F, S // 2, S, S, LANES), f32),
            pltpu.VMEM((S // 2, S, S, LANES), f32),
            padded,
            padded,
            pltpu.VMEM((S + 2, S + 2, S, LANES), f32),
            faces_x,
            faces_x,
            faces_y,
            faces_y,
            dma,
            dma,
        ],
        compiler_params=pltpu.CompilerParams(
            collective_id=1, has_side_effects=True, vmem_limit_bytes=VMEM_LIMIT
        ),
        name="sections",
    )(arrived, lane, walls, candidate, diffusivity, velocity)
    rows = pl.pallas_call(
        rows_kernel,
        out_shape=jax.ShapeDtypeStruct((F, patches, S * LAYER), f32),
        in_specs=vmem(2),
        out_specs=vmem(1)[0],
        compiler_params=pltpu.CompilerParams(vmem_limit_bytes=VMEM_LIMIT),
        name="rows",
    )(grid.reshape(F, LAYER * S, LANES), lane)
    return rows.transpose(1, 0, 2)


def solution(mesh):
    in_specs = (
        P(("gx", "gy"), None, None),
        P(("gx", "gy")),
        P(("gx", "gy"), None),
        P(("gx", "gy"), None, None),
        P(("gx", "gy"), None),
        P(),
        P(),
    )
    out_specs = P(("gx", "gy"), None, None)
    return jax.shard_map(
        per_device, mesh=mesh, in_specs=in_specs, out_specs=out_specs, check_vma=False
    )
```

```python
import functools

import jax
import jax.numpy as jnp
from jax import lax
from jax.experimental import pallas as pl
from jax.experimental.pallas import tpu as pltpu
from jax.sharding import PartitionSpec as P

S = 8
BX = 4
BY = 16
BZ = 2
SECTIONS = 4
F = 5
LANES = BX * BY * BZ
LAYER = S * S
CHUNKS = S * LAYER // LANES
VMEM_LIMIT = 56 * 1024 * 1024
MESH = pl.DeviceIdType.MESH
NN = (((1,), (0,)), ((), ()))
TN = (((0,), (0,)), ((), ()))
NT = (((1,), (1,)), ((), ()))


def iota(shape, axis):
    return lax.broadcasted_iota(jnp.int32, shape, axis)


def one_hot(mask):
    return jnp.where(mask, 1.0, 0.0).astype(jnp.bfloat16)


def parts(value):
    high = value.astype(jnp.bfloat16)
    rest = value - high.astype(jnp.float32)
    middle = rest.astype(jnp.bfloat16)
    low = (rest - middle.astype(jnp.float32)).astype(jnp.bfloat16)
    return high, middle, low


def pick(left, right, dims):
    def dot(a, b):
        return lax.dot_general(a, b, dims, preferred_element_type=jnp.float32)

    if left.dtype == jnp.float32:
        high, middle, low = (dot(part, right) for part in parts(left))
    else:
        high, middle, low = (dot(left, part) for part in parts(right))
    return high + middle + low


def roll(value, shift, axis):
    size = value.shape[axis]
    shift = shift % size
    return value if shift == 0 else pltpu.roll(value, shift, axis)


def column(row):
    wide = jnp.broadcast_to(row.astype(jnp.float32), (row.shape[1], row.shape[1]))
    return wide.T.astype(jnp.int32)


def slot_matrix(capacity, slots, row):
    patches = row.shape[1]
    bits = patches.bit_length() - 1
    dest_row = lax.shift_right_logical(row, bits)
    dest_col = lax.shift_right_logical(column(row), bits)
    square = (patches, patches)
    before = (dest_col == dest_row) & (iota(square, 0) < iota(square, 1))
    count = jnp.sum(jnp.where(before, 1, 0), axis=0, keepdims=True)
    return one_hot(iota((slots, patches), 0) == dest_row * capacity + count)


def pack(matrix, x_ref, send_ref, f):
    _, devices, _, capacity, _ = send_ref.shape
    moved = pick(matrix, x_ref[f], NN)
    for c in range(CHUNKS):
        part = moved[:, c * LANES : (c + 1) * LANES]
        send_ref[f, :, c] = part.reshape(devices, capacity, LANES)


def layers(coarse_ref, f):
    low = coarse_ref[f, :, :LANES]
    high = coarse_ref[f, :, (CHUNKS - 1) * LANES :]
    below = 1.25 * roll(high, LAYER, 1) - 0.25 * high
    above = 1.25 * roll(low, LAYER, 1) - 0.25 * low
    return jnp.where(iota(low.shape, 1) < LAYER, below, above)


def pack_kernel(x_ref, row_ref, coarse_ref, send_ref, wall_ref):
    _, devices, _, capacity, _ = send_ref.shape
    matrix = slot_matrix(capacity, devices * capacity, row_ref[...])
    for f in range(F):
        pack(matrix, x_ref, send_ref, f)
        wall_ref[f] = layers(coarse_ref, f)


def box_lane(box):
    across = lax.shift_right_logical(box, 4) & (BX - 1)
    return across * (BY * BZ) + lax.shift_right_logical(box, 6) * BY + (box & (BY - 1))


def local_kernel(recv_ref, rows_ref, wall_ref, *rest):
    sections(recv_ref, rows_ref, wall_ref, None, *rest)


def whole_kernel(
    x_ref, row_ref, coarse_ref, box_ref, source_ref, diff_ref, vel_ref, out_ref,
    send, recv, rows, wall, walls, send_sem, recv_sem, row_send, row_recv,
    wall_send, wall_recv, own_sem, *rest,
):
    gx, gy = lax.axis_index("gx"), lax.axis_index("gy")
    nx, ny = lax.axis_size("gx"), lax.axis_size("gy")
    devices = nx * ny
    capacity = send.shape[3]
    me = gx * ny + gy
    barrier = pltpu.get_barrier_semaphore()

    def partner(k):
        other = me ^ k
        return other, (lax.div(other, ny), lax.rem(other, ny))

    def each(body):
        def step(k, carry):
            body(k)
            return carry

        lax.fori_loop(1, devices, step, 0)

    def greet(k):
        pl.semaphore_signal(barrier, inc=1, device_id=partner(k)[1], device_id_type=MESH)

    each(greet)
    matrix = slot_matrix(capacity, devices * capacity, row_ref[...])
    pack(matrix, x_ref, send, 0)
    pl.semaphore_wait(barrier, devices - 1)

    def message(f, k):
        other, where = partner(k)
        return pltpu.make_async_remote_copy(
            src_ref=send.at[f, other],
            dst_ref=recv.at[f, me],
            send_sem=send_sem.at[f, k],
            recv_sem=recv_sem.at[f, k],
            device_id=where,
            device_id_type=MESH,
        )

    def row_message(k):
        return pltpu.make_async_remote_copy(
            src_ref=row_ref,
            dst_ref=rows.at[me],
            send_sem=row_send.at[k],
            recv_sem=row_recv.at[k],
            device_id=partner(k)[1],
            device_id_type=MESH,
        )

    def wall_message(k):
        return pltpu.make_async_remote_copy(
            src_ref=wall,
            dst_ref=walls.at[gx],
            send_sem=wall_send.at[k],
            recv_sem=wall_recv.at[k],
            device_id=(gx ^ k, gy),
            device_id_type=MESH,
        )

    def own(f):
        return pltpu.make_async_copy(send.at[f, me], recv.at[f, me], own_sem.at[f])

    own_row = pltpu.make_async_copy(row_ref, rows.at[me], own_sem.at[F])
    own_wall = pltpu.make_async_copy(wall, walls.at[gx], own_sem.at[F + 1])
    own_row.start()
    for f in range(F):
        if f:
            pack(matrix, x_ref, send, f)
        each(lambda k: message(f, k).start())
        own(f).start()
        if f == 0:
            each(lambda k: row_message(k).start())
            for g in range(F):
                wall[g] = layers(coarse_ref, g)
            for k in range(1, nx):
                wall_message(k).start()
            own_wall.start()

    def ready(what):
        if what == "rows":
            each(lambda k: row_message(k).wait())
            own_row.wait()
        elif what == "walls":
            for k in range(1, nx):
                wall_message(k).wait()
            own_wall.wait()
        else:
            each(lambda k: message(what, k).wait())
            own(what).wait()

    sections(
        recv, rows, walls, ready, box_ref, source_ref, diff_ref, vel_ref, out_ref, *rest
    )


def sections(
    recv_ref, rows_ref, wall_ref, ready, box_ref, source_ref, diff_ref, vel_ref, out_ref,
    cells, caps, cap_heat, grid_a, grid_b, heat,
    send_x, recv_x, send_y, recv_y, face_send, face_recv,
):
    gx, gy = lax.axis_index("gx"), lax.axis_index("gy")
    nx, ny = lax.axis_size("gx"), lax.axis_size("gy")
    me = gx * ny + gy
    right = (lax.rem(gx + 1, nx), gy)
    left = (lax.rem(gx + nx - 1, nx), gy)
    ahead = (gx, lax.rem(gy + 1, ny))
    behind = (gx, lax.rem(gy + ny - 1, ny))
    if ready is None:
        barrier = pltpu.get_barrier_semaphore()
        for other in (right, left, ahead, behind):
            pl.semaphore_signal(barrier, inc=1, device_id=other, device_id_type=MESH)
        pl.semaphore_wait(barrier, 4)

        def ready(what):
            return None

    _, devices, _, capacity, _ = recv_ref.shape
    slots = devices * capacity
    patches = LANES
    bits = patches.bit_length() - 1
    lane = iota((S, LANES), 1)
    by = lane & (BY - 1)
    bz = lax.shift_right_logical(lane, 4) & 1
    bx = lax.shift_right_logical(lane, 5)

    ready("walls")
    candidates = wall_ref.shape[0] * wall_ref.shape[2]
    need = wall_ref.shape[2]
    row_lane = iota((1, LANES), 1)
    entry = (
        (lax.shift_right_logical(row_lane, 4) & 1) * (need // 2)
        + lax.shift_right_logical(row_lane, 6) * (BY // 2)
        + lax.shift_right_logical(row_lane & (BY - 1), 1)
    )
    source = jnp.zeros((1, LANES), jnp.int32)
    for m in range(need):
        source = jnp.where(entry == m, source_ref[0, m], source)
    low_bits = need.bit_length() - 1
    owner = lax.shift_right_logical(source, low_bits + ny.bit_length() - 1)
    named = one_hot(iota((candidates, LANES), 0) == owner * need + (source & (need - 1)))
    odd_y = (row_lane & 1) == 1
    odd_x = (lax.shift_right_logical(row_lane, 5) & 1) == 1
    top = (lax.shift_right_logical(row_lane, 4) & 1) == 1
    for f in range(F):
        both = pick(wall_ref[:, f].reshape(candidates, LANES), named, TN)
        side = jnp.where(top, both[LAYER:], both[:LAYER])
        half = jnp.where(odd_x, side[LAYER // 2 :], side[: LAYER // 2])
        for j2 in range(S // 2):
            for k2 in range(S // 2):
                at = j2 * S + k2
                row = jnp.where(odd_y, half[at + 4 : at + 5], half[at : at + 1])
                full = jnp.broadcast_to(row, (S, LANES))
                caps[f, j2, 2 * k2] = full
                caps[f, j2, 2 * k2 + 1] = full
    cap_heat[...] = 1.0 + 0.5 * jnp.tanh(caps[0])
    for a in (0, S + 1):
        for b in (0, S + 1):
            grid_a[0, a, b] = jnp.zeros((S, LANES), jnp.float32)
            grid_b[0, a, b] = jnp.zeros((S, LANES), jnp.float32)

    ready("rows")
    senders = rows_ref[...].reshape(devices, LANES)
    sender = lax.shift_right_logical(iota((slots, devices), 0), capacity.bit_length() - 1)
    expand = one_hot(sender == iota((slots, devices), 1))
    places = pick(expand, senders.astype(jnp.float32), NN).astype(jnp.int32)
    mine = lax.shift_right_logical(places, bits) == me
    square = (LANES, LANES)
    earlier = lax.dot_general(
        one_hot(mine), one_hot(iota(square, 0) < iota(square, 1)), NN,
        preferred_element_type=jnp.float32,
    ).astype(jnp.int32)
    chosen = mine & (earlier == (iota((slots, LANES), 0) & (capacity - 1)))
    tag = jnp.sum(
        jnp.where(chosen, (places & (patches - 1)) + 1, 0), axis=1, keepdims=True
    )
    tagged = one_hot(tag == iota((slots, LANES), 1) + 1)
    boxed = one_hot(column(box_lane(box_ref[...])) == iota(square, 1))
    place = lax.dot_general(tagged, boxed, NN, preferred_element_type=jnp.float32)
    place = place.T.astype(jnp.bfloat16)
    for f in range(F):
        ready(f)
        for c in range(CHUNKS):
            part = recv_ref[f, :, c].reshape(slots, LANES)
            cells[f, c * LANES : (c + 1) * LANES, :] = pick(place, part, NN).T
        for jk in range(LAYER):
            grid_a[f, jk // S + 1, jk % S + 1] = cells[f, pl.ds(jk, S, stride=LAYER), :]

    started = []
    for section in range(SECTIONS):
        now, later = (grid_a, grid_b) if section % 2 == 0 else (grid_b, grid_a)
        copies = []

        def send(src, dst, way, target):
            copy = pltpu.make_async_remote_copy(
                src_ref=src.at[section, way % 2],
                dst_ref=dst.at[section, way % 2],
                send_sem=face_send.at[section, way],
                recv_sem=face_recv.at[section, way],
                device_id=target,
                device_id_type=MESH,
            )
            copy.start()
            copies.append(copy)
            started.append(copy)

        for way, line, edge, target in ((2, S, BY - 1, ahead), (3, 1, 0, behind)):
            for q in range(-(-F * S // BY)):
                packed = jnp.zeros((S, LANES), jnp.float32)
                for r in range(BY):
                    n = q * BY + r
                    if n < F * S:
                        face = now[n // S, n % S + 1, line]
                        packed = jnp.where(by == r, roll(face, r - edge, 1), packed)
                send_y[section, way - 2, q] = packed
            send(send_y, recv_y, way, target)
        for way, plane, edge, target in ((0, S, BX - 1, right), (1, 1, 0, left)):
            for f in range(F):
                for q in range(S // BX):
                    packed = jnp.zeros((S, LANES), jnp.float32)
                    for g in range(BX):
                        face = now[f, plane, q * BX + g + 1]
                        moved = roll(face, (g - edge) * BY * BZ, 1)
                        packed = jnp.where(bx == g, moved, packed)
                    send_x[section, way, f * (S // BX) + q] = packed
            send(send_x, recv_x, way, target)

        for order, (way, line, target_line, edge, step) in enumerate(
            ((0, S, 0, 0, 1), (1, 1, S + 1, BY - 1, -1))
        ):
            copies[order].wait_recv()
            for n in range(F * S):
                q, r = n // BY, n % BY
                remote = roll(recv_y[section, way, q], edge - r, 1)
                local = roll(now[n // S, n % S + 1, line], step, 1)
                now[n // S, n % S + 1, target_line] = jnp.where(by == edge, remote, local)
        for order, (way, plane, target_plane, edge, step) in enumerate(
            ((0, S, 0, 0, 1), (1, 1, S + 1, BX - 1, -1))
        ):
            copies[2 + order].wait_recv()
            for f in range(F):
                for k in range(S):
                    q, g = k // BX, k % BX
                    packed = recv_x[section, way, f * (S // BX) + q]
                    remote = roll(packed, (edge - g) * BY * BZ, 1)
                    local = roll(now[f, plane, k + 1], step * BY * BZ, 1)
                    now[f, target_plane, k + 1] = jnp.where(bx == edge, remote, local)

        def warm(j, carry):
            heat[j] = 1.0 + 0.5 * jnp.tanh(now[0, j])
            return carry

        lax.fori_loop(0, S + 2, warm, 0)

        box = (S, S, LANES)
        is_top = (iota(box, 1) == S - 1)
        is_bottom = (iota(box, 1) == 0)
        bz3 = lax.shift_right_logical(iota(box, 2), 4) & 1

        def neighbours(value, cap):
            rolled = roll(value, -1, 1)
            outer = jnp.where(bz3 == 0, roll(rolled, -BY, 2), cap)
            above = jnp.where(is_top, outer, rolled)
            rolled = roll(value, 1, 1)
            outer = jnp.where(bz3 == 1, roll(rolled, BY, 2), cap)
            below = jnp.where(is_bottom, outer, rolled)
            return above, below

        def pair(j2, carry):
            for jr in range(2):
                j = 2 * j2 + jr + 1
                inner = slice(1, S + 1)
                here = heat[j, inner]
                warm_z = neighbours(here, cap_heat[j2])
                warm_x = heat[j + 1, inner], heat[j - 1, inner]
                warm_y = heat[j, 2 : S + 2], heat[j, 0:S]
                means = [
                    (0.5 * (here + up), 0.5 * (here + down))
                    for up, down in (warm_z, warm_x, warm_y)
                ]
                for f in range(F):
                    u = now[f, j, inner]
                    around = (
                        neighbours(u, caps[f, j2]),
                        (now[f, j + 1, inner], now[f, j - 1, inner]),
                        (now[f, j, 2 : S + 2], now[f, j, 0:S]),
                    )
                    total = u
                    for axis in range(3):
                        up, down = around[axis]
                        mean_up, mean_down = means[axis]
                        v = vel_ref[axis]
                        total = total + (diff_ref[f] * mean_up - jnp.minimum(v, 0.0)) * (up - u)
                        total = total - (diff_ref[f] * mean_down + jnp.maximum(v, 0.0)) * (u - down)
                    if section == SECTIONS - 1:
                        out_ref[f, j - 1] = total
                    else:
                        later[f, j, inner] = total
            return carry

        lax.fori_loop(0, S // 2, pair, 0)
    for copy in started:
        copy.wait_send()


def rows_kernel(grid_ref, box_ref, out_ref):
    boxed = one_hot(column(box_lane(box_ref[...])) == iota((LANES, LANES), 1))
    for f in range(F):
        for c in range(CHUNKS):
            per = LANES // LAYER
            cells = jnp.concatenate(
                [grid_ref[f, pl.ds(c * per + i, LAYER, stride=S), :] for i in range(per)],
                axis=0,
            )
            out_ref[f, :, c * LANES : (c + 1) * LANES] = pick(boxed, cells, NT)


def vmem(count):
    return [pl.BlockSpec(memory_space=pltpu.VMEM)] * count


def per_device(
    fields_old, new_place, box_slot, coarse_fields, coarse_source, diffusivity, velocity
):
    devices = lax.axis_size(("gx", "gy"))
    mesh_x = lax.axis_size("gx")
    mesh_y = lax.axis_size("gy")
    patches = fields_old.shape[0]
    capacity = 2 * patches // devices
    need = coarse_source.shape[1]
    f32 = jnp.float32

    row = new_place.reshape(1, patches)
    operands = (fields_old.transpose(1, 0, 2), row, coarse_fields.transpose(1, 0, 2))
    shared = (box_slot, coarse_source, diffusivity, velocity)
    dma = pltpu.SemaphoreType.DMA
    padded = pltpu.VMEM((F, S + 2, S + 2, S, LANES), f32)
    faces_x = pltpu.VMEM((SECTIONS, 2, F * S // BX, S, LANES), f32)
    faces_y = pltpu.VMEM((SECTIONS, 2, -(-F * S // BY), S, LANES), f32)
    smem = pl.BlockSpec(memory_space=pltpu.SMEM)
    grid_shape = jax.ShapeDtypeStruct((F, S, S, S, LANES), f32)
    scratch = [
        pltpu.VMEM((F, S * LAYER, LANES), f32),
        pltpu.VMEM((F, S // 2, S, S, LANES), f32),
        pltpu.VMEM((S // 2, S, S, LANES), f32),
        padded,
        padded,
        pltpu.VMEM((S + 2, S + 2, S, LANES), f32),
        faces_x,
        faces_x,
        faces_y,
        faces_y,
        dma((SECTIONS, 4)),
        dma((SECTIONS, 4)),
    ]
    block = (F, devices, CHUNKS, capacity, LANES)
    params = pltpu.CompilerParams(
        collective_id=1, has_side_effects=True, vmem_limit_bytes=VMEM_LIMIT
    )
    if capacity % 8 == 0 and devices & (devices - 1) == 0 and mesh_x & (mesh_x - 1) == 0:
        grid = pl.pallas_call(
            whole_kernel,
            out_shape=grid_shape,
            in_specs=vmem(4) + [smem] * 3,
            out_specs=vmem(1)[0],
            scratch_shapes=[
                pltpu.VMEM(block, f32),
                pltpu.VMEM(block, f32),
                pltpu.VMEM((devices, 1, LANES), jnp.int32),
                pltpu.VMEM((F, need, LANES), f32),
                pltpu.VMEM((mesh_x, F, need, LANES), f32),
                dma((F, devices)),
                dma((F, devices)),
                dma((devices,)),
                dma((devices,)),
                dma((mesh_x,)),
                dma((mesh_x,)),
                dma((F + 2,)),
            ]
            + scratch,
            compiler_params=params,
            name="whole",
        )(*operands, *shared)
    else:
        packed, walls = pl.pallas_call(
            pack_kernel,
            out_shape=(
                jax.ShapeDtypeStruct(block, f32),
                jax.ShapeDtypeStruct((F, need, LANES), f32),
            ),
            in_specs=vmem(3),
            out_specs=tuple(vmem(2)),
            compiler_params=pltpu.CompilerParams(vmem_limit_bytes=VMEM_LIMIT),
            name="pack",
        )(*operands)
        arrived = lax.all_to_all(packed, ("gx", "gy"), split_axis=1, concat_axis=1, tiled=True)
        walls = lax.all_gather(walls, "gx", axis=0)
        rows_all = lax.all_gather(row, ("gx", "gy"), axis=0)
        grid = pl.pallas_call(
            local_kernel,
            out_shape=grid_shape,
            in_specs=vmem(4) + [smem] * 3,
            out_specs=vmem(1)[0],
            scratch_shapes=scratch,
            compiler_params=params,
            name="sections",
        )(arrived, rows_all, walls, *shared)
    rows = pl.pallas_call(
        rows_kernel,
        out_shape=jax.ShapeDtypeStruct((F, patches, S * LAYER), f32),
        in_specs=vmem(2),
        out_specs=vmem(1)[0],
        compiler_params=pltpu.CompilerParams(vmem_limit_bytes=VMEM_LIMIT),
        name="rows",
    )(grid.reshape(F, LAYER * S, LANES), box_slot)
    return rows.transpose(1, 0, 2)


def solution(mesh):
    in_specs = (
        P(("gx", "gy"), None, None),
        P(("gx", "gy")),
        P(("gx", "gy"), None),
        P(("gx", "gy"), None, None),
        P(("gx", "gy"), None),
        P(),
        P(),
    )
    out_specs = P(("gx", "gy"), None, None)
    return jax.shard_map(
        per_device, mesh=mesh, in_specs=in_specs, out_specs=out_specs, check_vma=False
    )
```

```python
import functools

import jax
import jax.numpy as jnp
from jax import lax
from jax.experimental import pallas as pl
from jax.experimental.pallas import tpu as pltpu
from jax.sharding import PartitionSpec as P

S = 8
BX = 4
BY = 16
BZ = 2
SECTIONS = 4
F = 5
LANES = BX * BY * BZ
LAYER = S * S
CHUNKS = S * LAYER // LANES
VMEM_LIMIT = 56 * 1024 * 1024
MESH = pl.DeviceIdType.MESH
NN = (((1,), (0,)), ((), ()))
TN = (((0,), (0,)), ((), ()))
NT = (((1,), (1,)), ((), ()))


def iota(shape, axis):
    return lax.broadcasted_iota(jnp.int32, shape, axis)


def one_hot(mask):
    return jnp.where(mask, 1.0, 0.0).astype(jnp.bfloat16)


def parts(value):
    high = value.astype(jnp.bfloat16)
    rest = value - high.astype(jnp.float32)
    middle = rest.astype(jnp.bfloat16)
    low = (rest - middle.astype(jnp.float32)).astype(jnp.bfloat16)
    return high, middle, low


def pick(left, right, dims):
    def dot(a, b):
        return lax.dot_general(a, b, dims, preferred_element_type=jnp.float32)

    if left.dtype == jnp.float32:
        high, middle, low = (dot(part, right) for part in parts(left))
    else:
        high, middle, low = (dot(left, part) for part in parts(right))
    return high + middle + low


def roll(value, shift, axis):
    size = value.shape[axis]
    shift = shift % size
    return value if shift == 0 else pltpu.roll(value, shift, axis)


def column(row):
    wide = jnp.broadcast_to(row.astype(jnp.float32), (row.shape[1], row.shape[1]))
    return wide.T.astype(jnp.int32)


def slot_matrix(capacity, slots, row):
    patches = row.shape[1]
    bits = patches.bit_length() - 1
    dest_row = lax.shift_right_logical(row, bits)
    dest_col = lax.shift_right_logical(column(row), bits)
    square = (patches, patches)
    before = (dest_col == dest_row) & (iota(square, 0) < iota(square, 1))
    count = jnp.sum(jnp.where(before, 1, 0), axis=0, keepdims=True)
    return one_hot(iota((slots, patches), 0) == dest_row * capacity + count)


def pack(matrix, x_ref, send_ref, f):
    _, devices, _, capacity, _ = send_ref.shape
    moved = pick(matrix, x_ref[f], NN)
    for c in range(CHUNKS):
        part = moved[:, c * LANES : (c + 1) * LANES]
        send_ref[f, :, c] = part.reshape(devices, capacity, LANES)


def layers(coarse_ref, f):
    low = coarse_ref[f, :, :LANES]
    high = coarse_ref[f, :, (CHUNKS - 1) * LANES :]
    below = 1.25 * roll(high, LAYER, 1) - 0.25 * high
    above = 1.25 * roll(low, LAYER, 1) - 0.25 * low
    return jnp.where(iota(low.shape, 1) < LAYER, below, above)


def pack_kernel(x_ref, row_ref, coarse_ref, send_ref, wall_ref):
    _, devices, _, capacity, _ = send_ref.shape
    matrix = slot_matrix(capacity, devices * capacity, row_ref[...])
    for f in range(F):
        pack(matrix, x_ref, send_ref, f)
        wall_ref[f] = layers(coarse_ref, f)


def box_lane(box):
    across = lax.shift_right_logical(box, 4) & (BX - 1)
    return across * (BY * BZ) + lax.shift_right_logical(box, 6) * BY + (box & (BY - 1))


def local_kernel(recv_ref, rows_ref, wall_ref, *rest):
    sections(recv_ref, rows_ref, wall_ref, None, *rest)


def whole_kernel(
    x_ref, row_ref, coarse_ref, box_ref, source_ref, diff_ref, vel_ref, out_ref,
    send, recv, rows, wall, walls, send_sem, recv_sem, row_send, row_recv,
    wall_send, wall_recv, own_sem, *rest,
):
    gx, gy = lax.axis_index("gx"), lax.axis_index("gy")
    nx, ny = lax.axis_size("gx"), lax.axis_size("gy")
    devices = nx * ny
    capacity = send.shape[3]
    me = gx * ny + gy
    barrier = pltpu.get_barrier_semaphore()

    def partner(k):
        other = me ^ k
        return other, (lax.div(other, ny), lax.rem(other, ny))

    def each(body):
        def step(k, carry):
            body(k)
            return carry

        lax.fori_loop(1, devices, step, 0)

    def greet(k):
        pl.semaphore_signal(barrier, inc=1, device_id=partner(k)[1], device_id_type=MESH)

    each(greet)
    matrix = slot_matrix(capacity, devices * capacity, row_ref[...])
    pack(matrix, x_ref, send, 0)
    pl.semaphore_wait(barrier, devices - 1)

    def message(f, k):
        other, where = partner(k)
        return pltpu.make_async_remote_copy(
            src_ref=send.at[f, other],
            dst_ref=recv.at[f, me],
            send_sem=send_sem.at[f, k],
            recv_sem=recv_sem.at[f, k],
            device_id=where,
            device_id_type=MESH,
        )

    def row_message(k):
        return pltpu.make_async_remote_copy(
            src_ref=row_ref,
            dst_ref=rows.at[me],
            send_sem=row_send.at[k],
            recv_sem=row_recv.at[k],
            device_id=partner(k)[1],
            device_id_type=MESH,
        )

    def wall_message(k):
        return pltpu.make_async_remote_copy(
            src_ref=wall,
            dst_ref=walls.at[gx],
            send_sem=wall_send.at[k],
            recv_sem=wall_recv.at[k],
            device_id=(gx ^ k, gy),
            device_id_type=MESH,
        )

    def own(f):
        return pltpu.make_async_copy(send.at[f, me], recv.at[f, me], own_sem.at[f])

    own_row = pltpu.make_async_copy(row_ref, rows.at[me], own_sem.at[F])
    own_wall = pltpu.make_async_copy(wall, walls.at[gx], own_sem.at[F + 1])
    own_row.start()
    for f in range(F):
        if f:
            pack(matrix, x_ref, send, f)
        each(lambda k: message(f, k).start())
        own(f).start()
        if f == 0:
            each(lambda k: row_message(k).start())
            for g in range(F):
                wall[g] = layers(coarse_ref, g)
            for k in range(1, nx):
                wall_message(k).start()
            own_wall.start()

    def ready(what):
        if what == "rows":
            each(lambda k: row_message(k).wait())
            own_row.wait()
        elif what == "walls":
            for k in range(1, nx):
                wall_message(k).wait()
            own_wall.wait()
        else:
            each(lambda k: message(what, k).wait())
            own(what).wait()

    sections(
        recv, rows, walls, ready, box_ref, source_ref, diff_ref, vel_ref, out_ref, *rest
    )


def sections(
    recv_ref, rows_ref, wall_ref, ready, box_ref, source_ref, diff_ref, vel_ref, out_ref,
    cells, caps, cap_heat, grid_a, grid_b, heat,
    send_x, recv_x, send_y, recv_y, face_send, face_recv,
):
    gx, gy = lax.axis_index("gx"), lax.axis_index("gy")
    nx, ny = lax.axis_size("gx"), lax.axis_size("gy")
    me = gx * ny + gy
    right = (lax.rem(gx + 1, nx), gy)
    left = (lax.rem(gx + nx - 1, nx), gy)
    ahead = (gx, lax.rem(gy + 1, ny))
    behind = (gx, lax.rem(gy + ny - 1, ny))
    if ready is None:
        barrier = pltpu.get_barrier_semaphore()
        for other in (right, left, ahead, behind):
            pl.semaphore_signal(barrier, inc=1, device_id=other, device_id_type=MESH)
        pl.semaphore_wait(barrier, 4)

        def ready(what):
            return None

    _, devices, _, capacity, _ = recv_ref.shape
    slots = devices * capacity
    patches = LANES
    bits = patches.bit_length() - 1
    lane = iota((S, LANES), 1)
    by = lane & (BY - 1)
    bz = lax.shift_right_logical(lane, 4) & 1
    bx = lax.shift_right_logical(lane, 5)

    ready("walls")
    candidates = wall_ref.shape[0] * wall_ref.shape[2]
    need = wall_ref.shape[2]
    row_lane = iota((1, LANES), 1)
    entry = (
        (lax.shift_right_logical(row_lane, 4) & 1) * (need // 2)
        + lax.shift_right_logical(row_lane, 6) * (BY // 2)
        + lax.shift_right_logical(row_lane & (BY - 1), 1)
    )
    source = jnp.zeros((1, LANES), jnp.int32)
    for m in range(need):
        source = jnp.where(entry == m, source_ref[0, m], source)
    low_bits = need.bit_length() - 1
    owner = lax.shift_right_logical(source, low_bits + ny.bit_length() - 1)
    named = one_hot(iota((candidates, LANES), 0) == owner * need + (source & (need - 1)))
    odd_y = (row_lane & 1) == 1
    odd_x = (lax.shift_right_logical(row_lane, 5) & 1) == 1
    top = (lax.shift_right_logical(row_lane, 4) & 1) == 1
    for f in range(F):
        both = pick(wall_ref[:, f].reshape(candidates, LANES), named, TN)
        side = jnp.where(top, both[LAYER:], both[:LAYER])
        half = jnp.where(odd_x, side[LAYER // 2 :], side[: LAYER // 2])
        for j2 in range(S // 2):
            for k2 in range(S // 2):
                at = j2 * S + k2
                row = jnp.where(odd_y, half[at + 4 : at + 5], half[at : at + 1])
                full = jnp.broadcast_to(row, (S, LANES))
                caps[f, j2, 2 * k2] = full
                caps[f, j2, 2 * k2 + 1] = full
    cap_heat[...] = 1.0 + 0.5 * jnp.tanh(caps[0])
    for a in (0, S + 1):
        for b in (0, S + 1):
            grid_a[0, a, b] = jnp.zeros((S, LANES), jnp.float32)
            grid_b[0, a, b] = jnp.zeros((S, LANES), jnp.float32)

    ready("rows")
    senders = rows_ref[...].reshape(devices, LANES)
    sender = lax.shift_right_logical(iota((slots, devices), 0), capacity.bit_length() - 1)
    expand = one_hot(sender == iota((slots, devices), 1))
    places = pick(expand, senders.astype(jnp.float32), NN).astype(jnp.int32)
    mine = lax.shift_right_logical(places, bits) == me
    square = (LANES, LANES)
    earlier = lax.dot_general(
        one_hot(mine), one_hot(iota(square, 0) < iota(square, 1)), NN,
        preferred_element_type=jnp.float32,
    ).astype(jnp.int32)
    chosen = mine & (earlier == (iota((slots, LANES), 0) & (capacity - 1)))
    tag = jnp.sum(
        jnp.where(chosen, (places & (patches - 1)) + 1, 0), axis=1, keepdims=True
    )
    tagged = one_hot(tag == iota((slots, LANES), 1) + 1)
    boxed = one_hot(column(box_lane(box_ref[...])) == iota(square, 1))
    place = lax.dot_general(tagged, boxed, NN, preferred_element_type=jnp.float32)
    place = place.T.astype(jnp.bfloat16)
    for f in range(F):
        ready(f)
        for c in range(CHUNKS):
            part = recv_ref[f, :, c].reshape(slots, LANES)
            cells[f, c * LANES : (c + 1) * LANES, :] = pick(place, part, NN).T
        for jk in range(LAYER):
            grid_a[f, jk // S + 1, jk % S + 1] = cells[f, pl.ds(jk, S, stride=LAYER), :]

    started = []
    for section in range(SECTIONS):
        now, later = (grid_a, grid_b) if section % 2 == 0 else (grid_b, grid_a)
        copies = []

        def send(src, dst, way, target):
            copy = pltpu.make_async_remote_copy(
                src_ref=src.at[section, way % 2],
                dst_ref=dst.at[section, way % 2],
                send_sem=face_send.at[section, way],
                recv_sem=face_recv.at[section, way],
                device_id=target,
                device_id_type=MESH,
            )
            copy.start()
            copies.append(copy)
            started.append(copy)

        for way, line, edge, target in ((2, S, BY - 1, ahead), (3, 1, 0, behind)):
            for q in range(-(-F * S // BY)):
                packed = jnp.zeros((S, LANES), jnp.float32)
                for r in range(BY):
                    n = q * BY + r
                    if n < F * S:
                        face = now[n // S, n % S + 1, line]
                        packed = jnp.where(by == r, roll(face, r - edge, 1), packed)
                send_y[section, way - 2, q] = packed
            send(send_y, recv_y, way, target)
        for way, plane, edge, target in ((0, S, BX - 1, right), (1, 1, 0, left)):
            for f in range(F):
                for q in range(S // BX):
                    packed = jnp.zeros((S, LANES), jnp.float32)
                    for g in range(BX):
                        face = now[f, plane, q * BX + g + 1]
                        moved = roll(face, (g - edge) * BY * BZ, 1)
                        packed = jnp.where(bx == g, moved, packed)
                    send_x[section, way, f * (S // BX) + q] = packed
            send(send_x, recv_x, way, target)

        for order, (way, line, target_line, edge, step) in enumerate(
            ((0, S, 0, 0, 1), (1, 1, S + 1, BY - 1, -1))
        ):
            copies[order].wait_recv()
            for n in range(F * S):
                q, r = n // BY, n % BY
                remote = roll(recv_y[section, way, q], edge - r, 1)
                local = roll(now[n // S, n % S + 1, line], step, 1)
                now[n // S, n % S + 1, target_line] = jnp.where(by == edge, remote, local)
        def warm(j, carry):
            heat[j] = 1.0 + 0.5 * jnp.tanh(now[0, j])
            return carry

        lax.fori_loop(1, S + 1, warm, 0)

        box = (S, S, LANES)
        is_top = (iota(box, 1) == S - 1)
        is_bottom = (iota(box, 1) == 0)
        bz3 = lax.shift_right_logical(iota(box, 2), 4) & 1

        def neighbours(value, cap):
            rolled = roll(value, -1, 1)
            outer = jnp.where(bz3 == 0, roll(rolled, -BY, 2), cap)
            above = jnp.where(is_top, outer, rolled)
            rolled = roll(value, 1, 1)
            outer = jnp.where(bz3 == 1, roll(rolled, BY, 2), cap)
            below = jnp.where(is_bottom, outer, rolled)
            return above, below

        def update(j, j2):
            inner = slice(1, S + 1)
            here = heat[j, inner]
            warm_z = neighbours(here, cap_heat[j2])
            warm_x = heat[j + 1, inner], heat[j - 1, inner]
            warm_y = heat[j, 2 : S + 2], heat[j, 0:S]
            means = [
                (0.5 * (here + up), 0.5 * (here + down))
                for up, down in (warm_z, warm_x, warm_y)
            ]
            for f in range(F):
                u = now[f, j, inner]
                around = (
                    neighbours(u, caps[f, j2]),
                    (now[f, j + 1, inner], now[f, j - 1, inner]),
                    (now[f, j, 2 : S + 2], now[f, j, 0:S]),
                )
                total = u
                for axis in range(3):
                    up, down = around[axis]
                    mean_up, mean_down = means[axis]
                    v = vel_ref[axis]
                    total = total + (diff_ref[f] * mean_up - jnp.minimum(v, 0.0)) * (up - u)
                    total = total - (diff_ref[f] * mean_down + jnp.maximum(v, 0.0)) * (u - down)
                if section == SECTIONS - 1:
                    out_ref[f, j - 1] = total
                else:
                    later[f, j, inner] = total

        def pair(t, carry):
            update(2 * t, t - 1)
            update(2 * t + 1, t)
            return carry

        lax.fori_loop(1, S // 2, pair, 0)
        for order, (way, plane, target_plane, edge, step) in enumerate(
            ((0, S, 0, 0, 1), (1, 1, S + 1, BX - 1, -1))
        ):
            copies[2 + order].wait_recv()
            for f in range(F):
                for k in range(S):
                    q, g = k // BX, k % BX
                    packed = recv_x[section, way, f * (S // BX) + q]
                    remote = roll(packed, (edge - g) * BY * BZ, 1)
                    local = roll(now[f, plane, k + 1], step * BY * BZ, 1)
                    now[f, target_plane, k + 1] = jnp.where(bx == edge, remote, local)

        warm(0, 0)
        warm(S + 1, 0)
        update(1, 0)
        update(S, S // 2 - 1)
    for copy in started:
        copy.wait_send()


def rows_kernel(grid_ref, box_ref, out_ref):
    boxed = one_hot(column(box_lane(box_ref[...])) == iota((LANES, LANES), 1))
    for f in range(F):
        for c in range(CHUNKS):
            per = LANES // LAYER
            cells = jnp.concatenate(
                [grid_ref[f, pl.ds(c * per + i, LAYER, stride=S), :] for i in range(per)],
                axis=0,
            )
            out_ref[f, :, c * LANES : (c + 1) * LANES] = pick(boxed, cells, NT)


def vmem(count):
    return [pl.BlockSpec(memory_space=pltpu.VMEM)] * count


def per_device(
    fields_old, new_place, box_slot, coarse_fields, coarse_source, diffusivity, velocity
):
    devices = lax.axis_size(("gx", "gy"))
    mesh_x = lax.axis_size("gx")
    mesh_y = lax.axis_size("gy")
    patches = fields_old.shape[0]
    capacity = 2 * patches // devices
    need = coarse_source.shape[1]
    f32 = jnp.float32

    row = new_place.reshape(1, patches)
    operands = (fields_old.transpose(1, 0, 2), row, coarse_fields.transpose(1, 0, 2))
    shared = (box_slot, coarse_source, diffusivity, velocity)
    dma = pltpu.SemaphoreType.DMA
    padded = pltpu.VMEM((F, S + 2, S + 2, S, LANES), f32)
    faces_x = pltpu.VMEM((SECTIONS, 2, F * S // BX, S, LANES), f32)
    faces_y = pltpu.VMEM((SECTIONS, 2, -(-F * S // BY), S, LANES), f32)
    smem = pl.BlockSpec(memory_space=pltpu.SMEM)
    grid_shape = jax.ShapeDtypeStruct((F, S, S, S, LANES), f32)
    scratch = [
        pltpu.VMEM((F, S * LAYER, LANES), f32),
        pltpu.VMEM((F, S // 2, S, S, LANES), f32),
        pltpu.VMEM((S // 2, S, S, LANES), f32),
        padded,
        padded,
        pltpu.VMEM((S + 2, S + 2, S, LANES), f32),
        faces_x,
        faces_x,
        faces_y,
        faces_y,
        dma((SECTIONS, 4)),
        dma((SECTIONS, 4)),
    ]
    block = (F, devices, CHUNKS, capacity, LANES)
    params = pltpu.CompilerParams(
        collective_id=1, has_side_effects=True, vmem_limit_bytes=VMEM_LIMIT
    )
    if capacity % 8 == 0 and devices & (devices - 1) == 0 and mesh_x & (mesh_x - 1) == 0:
        grid = pl.pallas_call(
            whole_kernel,
            out_shape=grid_shape,
            in_specs=vmem(4) + [smem] * 3,
            out_specs=vmem(1)[0],
            scratch_shapes=[
                pltpu.VMEM(block, f32),
                pltpu.VMEM(block, f32),
                pltpu.VMEM((devices, 1, LANES), jnp.int32),
                pltpu.VMEM((F, need, LANES), f32),
                pltpu.VMEM((mesh_x, F, need, LANES), f32),
                dma((F, devices)),
                dma((F, devices)),
                dma((devices,)),
                dma((devices,)),
                dma((mesh_x,)),
                dma((mesh_x,)),
                dma((F + 2,)),
            ]
            + scratch,
            compiler_params=params,
            name="whole",
        )(*operands, *shared)
    else:
        packed, walls = pl.pallas_call(
            pack_kernel,
            out_shape=(
                jax.ShapeDtypeStruct(block, f32),
                jax.ShapeDtypeStruct((F, need, LANES), f32),
            ),
            in_specs=vmem(3),
            out_specs=tuple(vmem(2)),
            compiler_params=pltpu.CompilerParams(vmem_limit_bytes=VMEM_LIMIT),
            name="pack",
        )(*operands)
        arrived = lax.all_to_all(packed, ("gx", "gy"), split_axis=1, concat_axis=1, tiled=True)
        walls = lax.all_gather(walls, "gx", axis=0)
        rows_all = lax.all_gather(row, ("gx", "gy"), axis=0)
        grid = pl.pallas_call(
            local_kernel,
            out_shape=grid_shape,
            in_specs=vmem(4) + [smem] * 3,
            out_specs=vmem(1)[0],
            scratch_shapes=scratch,
            compiler_params=params,
            name="sections",
        )(arrived, rows_all, walls, *shared)
    rows = pl.pallas_call(
        rows_kernel,
        out_shape=jax.ShapeDtypeStruct((F, patches, S * LAYER), f32),
        in_specs=vmem(2),
        out_specs=vmem(1)[0],
        compiler_params=pltpu.CompilerParams(vmem_limit_bytes=VMEM_LIMIT),
        name="rows",
    )(grid.reshape(F, LAYER * S, LANES), box_slot)
    return rows.transpose(1, 0, 2)


def solution(mesh):
    in_specs = (
        P(("gx", "gy"), None, None),
        P(("gx", "gy")),
        P(("gx", "gy"), None),
        P(("gx", "gy"), None, None),
        P(("gx", "gy"), None),
        P(),
        P(),
    )
    out_specs = P(("gx", "gy"), None, None)
    return jax.shard_map(
        per_device, mesh=mesh, in_specs=in_specs, out_specs=out_specs, check_vma=False
    )
```
